32 devices in a mesh: dp: 4 (over y, core), fsdp: 8 (over z, x).
Axes of the slice: x: 2, y: 2, z: 4, core: 2. Of those that a mesh axis runs over, the one named last changes fastest.
Arguments:
- tokens: bfloat16 [8, 1536, 1408], P('fsdp', 'dp')
- patches: int32 [8, 4, 4], P('fsdp', 'dp'), may hold values from 1 to 192, as said below
- owners: int32 [8, 4, 4], P('fsdp', 'dp'), may hold values from 0 to 3, as said below
- ln_gain: float32 [1408], replicated, may hold values from 0.5 to 1.5
- ln_shift: float32 [1408], replicated, may hold values from -2.5 to 2.5
- w_qkv: bfloat16 [1408, 4224], P('fsdp')
- b_qkv: float32 [4224], replicated, may hold values from -2.5 to 2.5
- w_proj: bfloat16 [1408, 1408], P('fsdp'), may hold values from -0.15625 to 0.15625
- b_proj: float32 [1408], replicated, may hold values from -3 to 3
- grad_out: bfloat16 [8, 1536, 1408], P('fsdp', 'dp'), may hold values from -6 to 6
Outputs:
- y_owned: bfloat16 [8, 1536, 1408], P('fsdp', 'dp')
- grad_tokens: bfloat16 [8, 1536, 1408], P('fsdp', 'dp')
- grad_qkv: float32 [1408, 4224], P('fsdp')
- grad_proj: float32 [1408, 1408], P('fsdp')
- grad_gain: float32 [1408], replicated
- grad_shift: float32 [1408], replicated
- grad_qkv_bias: float32 [4224], replicated
- grad_proj_bias: float32 [1408], replicated
The draws below stay inside these ranges and needn't reach their ends.
Inputs may be any that keep to these rules, and one draw needn't show every extreme that they name: The 4 images of each loader hold exactly 384 patches together; every dp group has an image of exactly 192 patches. Each loader sends exactly one image to each of the 4 owners of its dp group, so every owner receives exactly 384 patches.
All inputs are finite; a program needn't handle non-finite values.
Results may differ from the reference program's by a relative error of at most 0.024.
Values may be sent and summed in bfloat16 or wider, within the bound.
A program may use at most 192 MiB of HBM per device.

```python
from functools import partial
import jax
import jax.numpy as jnp
from jax import lax

D = 1408
HEADS = 16
LOAD = 384
MOST = 192
GROUP_ROWS = 1536
N_DP = 4
N_FSDP = 8


def plan_tables(key):
    others = N_DP - 1
    rest = LOAD - MOST
    pairs = others // 2
    reach = rest // others // 2

    def one_group(group_key):
        first, second, third, fourth = jax.random.split(group_key, 4)
        base_sizes = rest // others + (jnp.arange(others, dtype=jnp.int32) < rest % others).astype(jnp.int32)
        offsets = jax.random.randint(first, (pairs,), -reach, reach + 1, dtype=jnp.int32)
        middle = jnp.zeros((others - 2 * pairs,), jnp.int32)
        delta = jnp.concatenate([offsets, middle, -offsets[::-1]])
        image_sizes = jnp.concatenate([jnp.full((1,), MOST, jnp.int32), base_sizes + delta])
        shifts = jax.random.permutation(second, N_DP).astype(jnp.int32)
        relabel = jax.random.permutation(third, N_DP).astype(jnp.int32)
        orders = jax.vmap(lambda order_key: jax.random.permutation(order_key, N_DP))(jax.random.split(fourth, N_DP)).astype(jnp.int32)
        lengths = image_sizes[orders]
        loader_ids = jnp.arange(N_DP, dtype=jnp.int32)[:, None]
        targets = relabel[(loader_ids + shifts[orders]) % N_DP]
        return (lengths, targets)
    return jax.vmap(one_group)(jax.random.split(key, N_FSDP))


def draw_patches(key, part):
    tables = plan_tables(key)
    return tables[0]


def draw_owners(key, part):
    tables = plan_tables(key)
    return tables[1]


def draw_tokens(key, part):
    key = jax.random.fold_in(key, 3)
    first = jax.random.fold_in(key, 0)
    shape = (N_FSDP, N_DP * LOAD, D)
    values = jax.random.truncated_normal(first, -6.0, 6.0, shape, jnp.float32)
    return values.astype(jnp.bfloat16)


def draw_w_qkv(key, part):
    key = jax.random.fold_in(key, 5)
    shape = (D, 3 * D)
    values = jax.random.truncated_normal(key, -6.0, 6.0, shape, jnp.float32) * D ** (-0.5)
    return values.astype(jnp.bfloat16)


def levels(own_key, shape, cuts, smallest, high):
    def one(axis_at, shards_of):
        draws = jax.random.uniform(jax.random.fold_in(jax.random.fold_in(own_key, 6), axis_at), (shards_of,), jnp.float32, smallest / len(cuts), high / len(cuts))
        return jnp.repeat(jnp.exp(draws), shape[axis_at] // shards_of).reshape((-1,) + (1,) * (len(shape) - axis_at - 1))

    gain = one(*cuts[0])
    for cut in cuts[1:]:
        gain = gain * one(*cut)
    return gain


def scatter_about(rng, dims, deviation, most, shards=(), held_as=jnp.bfloat16):
    drawn = deviation * jax.random.normal(rng, dims, jnp.float32)
    if shards:
        drawn = drawn * levels(rng, dims, shards, -0.22, 0.18)
    return jnp.clip(drawn, -most, most).astype(held_as)


def setup_inputs(seed: int = 0) -> dict:
    splits = jax.random.split(jax.random.key(seed), 11)
    tokens = draw_tokens(jax.random.fold_in(splits[10], 71), 0)
    patches = draw_patches(jax.random.fold_in(splits[10], 71), 0)
    owners = draw_owners(jax.random.fold_in(splits[10], 71), 0)
    ln_gain = jnp.clip(1.0 + 0.1 * jax.random.normal(splits[3], (D,), jnp.float32), 0.5, 1.5)
    ln_shift = scatter_about(splits[4], (D,), 0.3, 2.5, (), jnp.float32)
    w_qkv = draw_w_qkv(jax.random.fold_in(splits[10], 71), 0)
    b_qkv = scatter_about(splits[6], (3 * D,), 0.3, 2.5, (), jnp.float32)
    w_proj = scatter_about(splits[7], (D, D), D ** -0.5, 0.15625, ((0, 8),))
    b_proj = scatter_about(splits[8], (D,), 0.5, 3.0, (), jnp.float32)
    grad_out = scatter_about(splits[9], (N_FSDP, GROUP_ROWS, D), 1.0, 6.0, ((0, 8), (1, 4)))
    return {"tokens": tokens, "patches": patches, "owners": owners, "ln_gain": ln_gain, "ln_shift": ln_shift, "w_qkv": w_qkv, "b_qkv": b_qkv, "w_proj": w_proj, "b_proj": b_proj, "grad_out": grad_out}


NEG_FILL = -1e+30
LN_EPS = 1e-06

def attention_layer(segments, owned_rows, ln_gain, ln_shift, w_qkv, b_qkv, w_proj, b_proj):
    row_count, model_width = owned_rows.shape
    head_size = model_width // HEADS
    inputs = owned_rows.astype(jnp.float32)
    centre = lax.optimization_barrier(jnp.mean(inputs, axis=1, keepdims=True))
    spread = lax.optimization_barrier(jnp.mean(jnp.square(inputs - centre), axis=1, keepdims=True))
    normed = ((inputs - centre) * lax.rsqrt(spread + LN_EPS) * ln_gain + ln_shift).astype(jnp.bfloat16)
    joined = (jnp.dot(normed, w_qkv, preferred_element_type=jnp.float32) + b_qkv).astype(jnp.bfloat16)
    queries = joined[:, :model_width].reshape(row_count, HEADS, head_size).astype(jnp.float32)
    keys_all = joined[:, model_width:2 * model_width].reshape(row_count, HEADS, head_size).astype(jnp.float32)
    values_all = joined[:, 2 * model_width:].reshape(row_count, HEADS, head_size).astype(jnp.float32)
    scores = jnp.einsum('qhd,khd->hqk', queries, keys_all) * head_size ** (-0.5)
    same_image = segments[:, None] == segments[None, :]
    scores = jnp.where(same_image[None], scores, NEG_FILL)
    row_peak = lax.stop_gradient(lax.optimization_barrier(jnp.max(scores, axis=2, keepdims=True)))
    exp_scores = jnp.exp(scores - row_peak)
    attention_weights = (exp_scores / lax.optimization_barrier(jnp.sum(exp_scores, axis=2, keepdims=True))).astype(jnp.bfloat16)
    context = jnp.einsum('hqk,khd->qhd', attention_weights.astype(jnp.float32), values_all)
    context = context.reshape(row_count, model_width).astype(jnp.bfloat16)
    layer_out = jnp.dot(context, w_proj, preferred_element_type=jnp.float32) + b_proj + inputs
    return layer_out.astype(jnp.bfloat16)

def owner_rows(lengths, targets):
    peer_ids = jnp.arange(N_DP, dtype=jnp.int32)
    slot_start = (jnp.cumsum(lengths, axis=1) - lengths).astype(jnp.int32)
    slot_end = (slot_start + lengths).astype(jnp.int32)
    owner_hits = (targets[:, :, None] == peer_ids[None, None, :]).astype(jnp.int32)
    pair_length = lax.optimization_barrier(jnp.sum(lengths[:, :, None] * owner_hits, axis=1)).astype(jnp.int32)
    pair_offset = (jnp.cumsum(pair_length, axis=0) - pair_length).astype(jnp.int32)
    slot_offset = lax.optimization_barrier(jnp.sum(owner_hits * pair_offset[:, None, :], axis=2)).astype(jnp.int32)
    positions = jnp.arange(LOAD, dtype=jnp.int32)
    slot_of_row = lax.optimization_barrier(jnp.sum((positions[None, :, None] >= slot_end[:, None, :]).astype(jnp.int32), axis=2)).astype(jnp.int32)
    row_owner = jnp.take_along_axis(targets, slot_of_row, axis=1)
    row_offset = jnp.take_along_axis(slot_offset, slot_of_row, axis=1)
    row_start = jnp.take_along_axis(slot_start, slot_of_row, axis=1)
    destination = row_owner * LOAD + row_offset + positions[None, :] - row_start
    return destination.reshape(N_DP * LOAD).astype(jnp.int32)

def reference(tokens, patches, owners, ln_gain, ln_shift, w_qkv, b_qkv, w_proj, b_proj, grad_out):
    destination = jax.vmap(owner_rows)(patches, owners)
    group_rows = N_DP * LOAD
    model_width = tokens.shape[2]
    owner_count = N_FSDP * N_DP
    source_loader = jnp.repeat(jnp.arange(N_DP, dtype=jnp.int32), LOAD)
    owned = jax.vmap(lambda data_rows, target: jnp.zeros_like(data_rows).at[target].set(data_rows))(tokens, destination)
    segments = jax.vmap(lambda target: jnp.zeros((group_rows,), jnp.int32).at[target].set(source_loader))(destination)
    blocks = (owned.reshape(owner_count, LOAD, model_width), segments.reshape(owner_count, LOAD), grad_out.reshape(owner_count, LOAD, model_width))

    def one_owner(running, owner_block):
        block_rows, block_segments, block_cotangent = owner_block
        layer_out, backward = jax.vjp(partial(attention_layer, block_segments), block_rows, ln_gain, ln_shift, w_qkv, b_qkv, w_proj, b_proj)
        gradients = backward(block_cotangent)
        running = tuple((held_sum + term_part.astype(jnp.float32) for held_sum, term_part in zip(running, gradients[1:])))
        return (running, (layer_out, gradients[0]))
    zero_sums = tuple((jnp.zeros(param_array.shape, jnp.float32) for param_array in (ln_gain, ln_shift, w_qkv, b_qkv, w_proj, b_proj)))
    totals, (outputs, grad_owned) = lax.scan(one_owner, zero_sums, blocks)
    y_owned = outputs.reshape(N_FSDP, group_rows, model_width)
    grad_owned = grad_owned.reshape(N_FSDP, group_rows, model_width)
    grad_tokens = jax.vmap(lambda data_rows, target: data_rows[target])(grad_owned, destination)
    device_share = 1.0 / owner_count
    return (y_owned, grad_tokens, totals[2] * device_share, totals[4] * device_share, totals[0] * device_share, totals[1] * device_share, totals[3] * device_share, totals[5] * device_share)
```

```python
from functools import partial

import jax
import jax.numpy as jnp
from jax import lax
from jax.sharding import PartitionSpec as P

HEADS = 16


NEG_FILL = -1e30
LN_EPS = 1e-06


def layer_norm(rows, ln_gain, ln_shift):
    inputs = rows.astype(jnp.float32)
    centre = jnp.mean(inputs, axis=1, keepdims=True)
    spread = jnp.mean(jnp.square(inputs - centre), axis=1, keepdims=True)
    normed = ((inputs - centre) * lax.rsqrt(spread + LN_EPS) * ln_gain + ln_shift).astype(
        jnp.bfloat16
    )
    return normed, inputs


def attend(same_image, head_count, joined):
    loaders, row_count, _ = same_image.shape
    width = joined.shape[1] // 3
    head_size = width // head_count

    def heads_of(part):
        return part.reshape(loaders, row_count, head_count, head_size).astype(jnp.float32)

    queries = heads_of(joined[:, :width])
    keys = heads_of(joined[:, width : 2 * width])
    values = heads_of(joined[:, 2 * width :])
    scores = jnp.einsum("aqhd,akhd->ahqk", queries, keys) * head_size ** (-0.5)
    scores = jnp.where(same_image[:, None], scores, NEG_FILL)
    row_peak = lax.stop_gradient(jnp.max(scores, axis=3, keepdims=True))
    exp_scores = jnp.exp(scores - row_peak)
    weights = (exp_scores / jnp.sum(exp_scores, axis=3, keepdims=True)).astype(jnp.bfloat16)
    context = jnp.einsum("ahqk,akhd->aqhd", weights.astype(jnp.float32), values)
    return context.reshape(loaders * row_count, width).astype(jnp.bfloat16)


def per_device(tokens, patches, owners, ln_gain, ln_shift, w_qkv, b_qkv, w_proj, b_proj, grad_out):
    own_tokens = tokens[0]
    row_count, model_width = own_tokens.shape
    dp_size = lax.axis_size("dp")
    fsdp_size = lax.axis_size("fsdp")
    me = lax.axis_index("dp")
    shard = lax.axis_index("fsdp")
    head_count = HEADS // dp_size
    width = model_width // dp_size
    shard_rows = w_qkv.shape[0]

    w_part = jnp.concatenate(
        [
            lax.dynamic_slice_in_dim(w_qkv, part * model_width + me * width, width, 1)
            for part in range(3)
        ],
        axis=1,
    )
    b_part = lax.dynamic_slice_in_dim(b_qkv.reshape(3, dp_size, width), me, 1, axis=1).reshape(-1)

    all_tokens = lax.all_gather(own_tokens, "dp", axis=0, tiled=True)
    w_heads = lax.all_gather(w_part, "fsdp", axis=0, tiled=True)
    all_grad = lax.all_gather(grad_out[0], "dp", axis=0, tiled=True)
    w_full = lax.all_gather(w_proj, "fsdp", axis=0, tiled=True)
    tables = lax.all_gather(
        jnp.concatenate([patches, owners], axis=2), "dp", axis=1, tiled=True
    )[0]
    lengths, targets = tables[:, :dp_size], tables[:, dp_size:]

    positions = jnp.arange(row_count, dtype=jnp.int32)
    peers = jnp.arange(dp_size, dtype=jnp.int32)
    slot_start = jnp.cumsum(lengths, axis=1) - lengths
    slot_end = slot_start + lengths
    hits = (targets[:, :, None] == peers).astype(jnp.int32)
    pair_length = jnp.sum(lengths[:, :, None] * hits, axis=1)
    pair_start = jnp.sum(slot_start[:, :, None] * hits, axis=1)
    pair_offset = jnp.cumsum(pair_length, axis=0) - pair_length
    slot_base = (
        targets * row_count + jnp.sum(hits * pair_offset[:, None, :], axis=2) - slot_start
    )
    image = jnp.sum((positions[None, :, None] >= slot_end[:, None, :]).astype(jnp.int32), axis=2)
    image_hit = (image[:, :, None] == peers).astype(jnp.int32)
    destination = (
        jnp.sum(image_hit * slot_base[:, None, :], axis=2) + positions[None, :]
    ).reshape(-1)
    same_image = image[:, :, None] == image[:, None, :]
    pair_end = pair_offset + pair_length
    source = jnp.sum(
        (positions[None, :, None] >= pair_end.T[:, None, :]).astype(jnp.int32), axis=2
    )
    source_hit = (source[:, :, None] == peers).astype(jnp.int32)
    pair_base = (peers[:, None] * row_count + pair_start - pair_offset).T
    origin = jnp.sum(source_hit * pair_base[:, None, :], axis=2) + positions[None, :]

    normed, _ = layer_norm(all_tokens, ln_gain, ln_shift)
    joined = (jnp.dot(normed, w_heads, preferred_element_type=jnp.float32) + b_part).astype(
        jnp.bfloat16
    )
    context, attend_back = jax.vjp(partial(attend, same_image, head_count), joined)
    grad_rows = all_grad[destination]
    w_rows = lax.dynamic_slice_in_dim(w_full, me * width, width, 0)
    grad_context = lax.dot_general(
        grad_rows, w_rows, (((1,), (1,)), ((), ())), preferred_element_type=jnp.float32
    ).astype(jnp.bfloat16)
    (grad_joined,) = attend_back(grad_context)

    term_proj = lax.dot_general(
        context, grad_rows, (((0,), (0,)), ((), ())), preferred_element_type=jnp.float32
    ).astype(jnp.bfloat16)
    rows_proj = lax.psum(term_proj, "fsdp")
    per_block = width // shard_rows
    mine = lax.dynamic_slice_in_dim(rows_proj, (shard % per_block) * shard_rows, shard_rows, 0)
    mine = jnp.where(shard // per_block == me, mine, jnp.zeros((), mine.dtype))
    summed_proj = lax.psum(mine, "dp")

    term_qkv = lax.dot_general(
        normed, grad_joined, (((0,), (0,)), ((), ())), preferred_element_type=jnp.float32
    ).astype(jnp.bfloat16)
    shard_qkv = lax.psum_scatter(term_qkv, "fsdp", scatter_dimension=0, tiled=True)
    all_qkv = lax.all_gather(shard_qkv, "dp", axis=0)
    summed_qkv = jnp.concatenate(
        [
            all_qkv[peer, :, part * width : (part + 1) * width]
            for part in range(3)
            for peer in range(dp_size)
        ],
        axis=1,
    )

    part_normed = lax.dot_general(
        grad_joined, w_heads, (((1,), (1,)), ((), ())), preferred_element_type=jnp.float32
    ).astype(jnp.bfloat16)
    parts = lax.all_to_all(
        part_normed.reshape(dp_size, row_count, model_width), "dp", 0, 0, tiled=True
    )
    grad_normed = jnp.sum(parts.astype(jnp.float32), axis=0).astype(jnp.bfloat16)
    own_grad = lax.dynamic_slice_in_dim(grad_rows, me * row_count, row_count, 0).astype(
        jnp.float32
    )
    _, norm_back = jax.vjp(layer_norm, own_tokens, ln_gain, ln_shift)
    grad_tokens, gain_term, shift_term = norm_back((grad_normed, own_grad))

    context_out = lax.all_to_all(
        context[origin.reshape(-1)].reshape(dp_size, row_count, width), "dp", 0, 0, tiled=True
    )
    own_context = jnp.concatenate([context_out[peer] for peer in range(dp_size)], axis=1)
    own_origin = lax.dynamic_slice_in_dim(origin, me, 1, 0)[0]
    owned = all_tokens[own_origin].astype(jnp.float32)
    y_owned = (
        jnp.dot(own_context, w_full, preferred_element_type=jnp.float32) + b_proj + owned
    ).astype(jnp.bfloat16)

    bias_part = jnp.sum(grad_joined.astype(jnp.float32), axis=0).reshape(3, 1, width)
    bias_term = jnp.where(
        peers[None, :, None] == me, bias_part, jnp.zeros((), jnp.float32)
    ).reshape(-1)
    proj_term = jnp.sum(grad_out[0].astype(jnp.float32), axis=0)
    small = lax.all_gather(
        jnp.concatenate([gain_term, shift_term, bias_term, proj_term]), ("dp", "fsdp")
    )
    device_share = 1.0 / (dp_size * fsdp_size)
    small = jnp.sum(small, axis=0) * device_share
    cuts = (model_width, 2 * model_width, 5 * model_width)
    gain, shift, qkv_bias, proj_bias = jnp.split(small, cuts)
    return (
        y_owned[None],
        grad_tokens[None],
        summed_qkv.astype(jnp.float32) * device_share,
        summed_proj.astype(jnp.float32) * device_share,
        gain,
        shift,
        qkv_bias,
        proj_bias,
    )


def solution(mesh):
    placed = (
        P("fsdp", "dp", None),
        P("fsdp", "dp", None),
        P("fsdp", "dp", None),
        P(),
        P(),
        P("fsdp", None),
        P(),
        P("fsdp", None),
        P(),
        P("fsdp", "dp", None),
    )
    return jax.shard_map(
        per_device,
        mesh=mesh,
        in_specs=placed,
        out_specs=(
            P("fsdp", "dp", None),
            P("fsdp", "dp", None),
            P("fsdp", None),
            P("fsdp", None),
            P(),
            P(),
            P(),
            P(),
        ),
        check_vma=False,
    )
```

```python
from functools import partial

import jax
import jax.numpy as jnp
from jax import lax
from jax.sharding import PartitionSpec as P

HEADS = 16


NEG_FILL = -1e30
LN_EPS = 1e-06


def layer_norm(rows, ln_gain, ln_shift):
    inputs = rows.astype(jnp.float32)
    centre = jnp.mean(inputs, axis=1, keepdims=True)
    spread = jnp.mean(jnp.square(inputs - centre), axis=1, keepdims=True)
    normed = ((inputs - centre) * lax.rsqrt(spread + LN_EPS) * ln_gain + ln_shift).astype(
        jnp.bfloat16
    )
    return normed, inputs


def attend(same_image, head_count, joined):
    loaders, row_count, _ = same_image.shape
    width = joined.shape[1] // 3
    head_size = width // head_count

    def heads_of(part):
        return part.reshape(loaders, row_count, head_count, head_size).astype(jnp.float32)

    queries = heads_of(joined[:, :width])
    keys = heads_of(joined[:, width : 2 * width])
    values = heads_of(joined[:, 2 * width :])
    scores = jnp.einsum("aqhd,akhd->ahqk", queries, keys) * head_size ** (-0.5)
    scores = jnp.where(same_image[:, None], scores, NEG_FILL)
    row_peak = lax.stop_gradient(jnp.max(scores, axis=3, keepdims=True))
    exp_scores = jnp.exp(scores - row_peak)
    weights = (exp_scores / jnp.sum(exp_scores, axis=3, keepdims=True)).astype(jnp.bfloat16)
    context = jnp.einsum("ahqk,akhd->aqhd", weights.astype(jnp.float32), values)
    return context.reshape(loaders * row_count, width).astype(jnp.bfloat16)


def to_group(rows, dp_size):
    copies = jnp.broadcast_to(rows[None], (dp_size,) + rows.shape)
    return lax.all_to_all(copies, "dp", 0, 0, tiled=True).reshape(-1, rows.shape[1])


def per_device(tokens, patches, owners, ln_gain, ln_shift, w_qkv, b_qkv, w_proj, b_proj, grad_out):
    own_tokens = tokens[0]
    row_count, model_width = own_tokens.shape
    dp_size = lax.axis_size("dp")
    fsdp_size = lax.axis_size("fsdp")
    me = lax.axis_index("dp")
    shard = lax.axis_index("fsdp")
    head_count = HEADS // dp_size
    width = model_width // dp_size
    shard_rows = w_qkv.shape[0]

    w_part = jnp.concatenate(
        [
            lax.dynamic_slice_in_dim(w_qkv, part * model_width + me * width, width, 1)
            for part in range(3)
        ],
        axis=1,
    )
    b_part = lax.dynamic_slice_in_dim(b_qkv.reshape(3, dp_size, width), me, 1, axis=1).reshape(-1)

    piece_rows = shard_rows // dp_size
    per_block = width // shard_rows
    to_heads = [
        (d * fsdp_size + f, (f // per_block) * fsdp_size + (f % per_block) * dp_size + d)
        for d in range(dp_size)
        for f in range(fsdp_size)
    ]
    to_shards = [(there, here) for here, there in to_heads]
    own_piece = lax.dynamic_index_in_dim(
        w_proj.reshape(dp_size, piece_rows, model_width), me, 0, keepdims=False
    )
    head_piece = lax.ppermute(own_piece, ("dp", "fsdp"), to_heads)

    all_tokens = to_group(own_tokens, dp_size)
    w_heads = lax.all_gather(w_part, "fsdp", axis=0, tiled=True)
    all_grad = to_group(grad_out[0], dp_size)
    w_rows = lax.all_gather(head_piece, "fsdp", axis=0).reshape(width, model_width)
    tables = lax.all_gather(
        jnp.concatenate([patches, owners], axis=2), "dp", axis=1, tiled=True
    )[0]
    lengths, targets = tables[:, :dp_size], tables[:, dp_size:]

    positions = jnp.arange(row_count, dtype=jnp.int32)
    peers = jnp.arange(dp_size, dtype=jnp.int32)
    slot_start = jnp.cumsum(lengths, axis=1) - lengths
    slot_end = slot_start + lengths
    hits = (targets[:, :, None] == peers).astype(jnp.int32)
    pair_length = jnp.sum(lengths[:, :, None] * hits, axis=1)
    pair_start = jnp.sum(slot_start[:, :, None] * hits, axis=1)
    pair_offset = jnp.cumsum(pair_length, axis=0) - pair_length
    slot_base = (
        targets * row_count + jnp.sum(hits * pair_offset[:, None, :], axis=2) - slot_start
    )
    image = jnp.sum((positions[None, :, None] >= slot_end[:, None, :]).astype(jnp.int32), axis=2)
    image_hit = (image[:, :, None] == peers).astype(jnp.int32)
    destination = (
        jnp.sum(image_hit * slot_base[:, None, :], axis=2) + positions[None, :]
    ).reshape(-1)
    same_image = image[:, :, None] == image[:, None, :]
    pair_end = pair_offset + pair_length
    source = jnp.sum(
        (positions[None, :, None] >= pair_end.T[:, None, :]).astype(jnp.int32), axis=2
    )
    source_hit = (source[:, :, None] == peers).astype(jnp.int32)
    pair_base = (peers[:, None] * row_count + pair_start - pair_offset).T
    origin = jnp.sum(source_hit * pair_base[:, None, :], axis=2) + positions[None, :]

    normed, _ = layer_norm(all_tokens, ln_gain, ln_shift)
    joined = (jnp.dot(normed, w_heads, preferred_element_type=jnp.float32) + b_part).astype(
        jnp.bfloat16
    )
    context, attend_back = jax.vjp(partial(attend, same_image, head_count), joined)
    grad_rows = all_grad[destination]
    grad_context = lax.dot_general(
        grad_rows, w_rows, (((1,), (1,)), ((), ())), preferred_element_type=jnp.float32
    ).astype(jnp.bfloat16)
    (grad_joined,) = attend_back(grad_context)

    term_proj = lax.dot_general(
        context, grad_rows, (((0,), (0,)), ((), ())), preferred_element_type=jnp.float32
    ).astype(jnp.bfloat16)
    pieces = lax.all_to_all(
        term_proj.reshape(fsdp_size, piece_rows, model_width), "fsdp", 0, 0, tiled=True
    )
    piece_proj = jnp.sum(pieces.astype(jnp.float32), axis=0).astype(jnp.bfloat16)
    piece_proj = lax.ppermute(piece_proj, ("dp", "fsdp"), to_shards)

    term_qkv = lax.dot_general(
        normed, grad_joined, (((0,), (0,)), ((), ())), preferred_element_type=jnp.float32
    ).astype(jnp.bfloat16)
    shard_qkv = lax.psum_scatter(term_qkv, "fsdp", scatter_dimension=0, tiled=True)
    sums = jnp.concatenate([shard_qkv, piece_proj.reshape(shard_rows, width)], axis=1)
    all_sums = lax.all_gather(sums, "dp", axis=0)
    all_qkv = all_sums[:, :, : 3 * width]
    summed_proj = all_sums[:, :, 3 * width :].reshape(shard_rows, model_width)
    summed_qkv = jnp.concatenate(
        [
            all_qkv[peer, :, part * width : (part + 1) * width]
            for part in range(3)
            for peer in range(dp_size)
        ],
        axis=1,
    )

    part_normed = lax.dot_general(
        grad_joined, w_heads, (((1,), (1,)), ((), ())), preferred_element_type=jnp.float32
    ).astype(jnp.bfloat16)
    parts = lax.all_to_all(
        part_normed.reshape(dp_size, row_count, model_width), "dp", 0, 0, tiled=True
    )
    grad_normed = jnp.sum(parts.astype(jnp.float32), axis=0).astype(jnp.bfloat16)
    own_grad = lax.dynamic_slice_in_dim(grad_rows, me * row_count, row_count, 0).astype(
        jnp.float32
    )
    _, norm_back = jax.vjp(layer_norm, own_tokens, ln_gain, ln_shift)
    grad_tokens, gain_term, shift_term = norm_back((grad_normed, own_grad))

    part_out = jnp.dot(
        context[origin.reshape(-1)], w_rows, preferred_element_type=jnp.float32
    ).astype(jnp.bfloat16)
    parts_out = lax.all_to_all(
        part_out.reshape(dp_size, row_count, model_width), "dp", 0, 0, tiled=True
    )
    own_origin = lax.dynamic_slice_in_dim(origin, me, 1, 0)[0]
    owned = all_tokens[own_origin].astype(jnp.float32)
    y_owned = (jnp.sum(parts_out.astype(jnp.float32), axis=0) + b_proj + owned).astype(
        jnp.bfloat16
    )

    bias_part = jnp.sum(grad_joined.astype(jnp.float32), axis=0).reshape(3, 1, width)
    bias_term = jnp.where(
        peers[None, :, None] == me, bias_part, jnp.zeros((), jnp.float32)
    ).reshape(-1)
    proj_term = jnp.sum(grad_out[0].astype(jnp.float32), axis=0)
    terms = jnp.concatenate([gain_term, shift_term, bias_term, proj_term])
    spread = lax.all_to_all(
        terms.reshape(dp_size * fsdp_size, -1), ("dp", "fsdp"), 0, 0, tiled=True
    )
    device_share = 1.0 / (dp_size * fsdp_size)
    share = jnp.sum(spread, axis=0, keepdims=True) * device_share
    small = lax.all_to_all(
        jnp.broadcast_to(share, spread.shape), ("dp", "fsdp"), 0, 0, tiled=True
    ).reshape(-1)
    cuts = (model_width, 2 * model_width, 5 * model_width)
    gain, shift, qkv_bias, proj_bias = jnp.split(small, cuts)
    return (
        y_owned[None],
        grad_tokens[None],
        summed_qkv.astype(jnp.float32) * device_share,
        summed_proj.astype(jnp.float32) * device_share,
        gain,
        shift,
        qkv_bias,
        proj_bias,
    )


def solution(mesh):
    placed = (
        P("fsdp", "dp", None),
        P("fsdp", "dp", None),
        P("fsdp", "dp", None),
        P(),
        P(),
        P("fsdp", None),
        P(),
        P("fsdp", None),
        P(),
        P("fsdp", "dp", None),
    )
    return jax.shard_map(
        per_device,
        mesh=mesh,
        in_specs=placed,
        out_specs=(
            P("fsdp", "dp", None),
            P("fsdp", "dp", None),
            P("fsdp", None),
            P("fsdp", None),
            P(),
            P(),
            P(),
            P(),
        ),
        check_vma=False,
    )
```

```python
from functools import partial

import jax
import jax.numpy as jnp
from jax import lax
from jax.sharding import PartitionSpec as P

HEADS = 16


NEG_FILL = -1e30
LN_EPS = 1e-06


def layer_norm(rows, ln_gain, ln_shift):
    inputs = rows.astype(jnp.float32)
    centre = jnp.mean(inputs, axis=1, keepdims=True)
    spread = jnp.mean(jnp.square(inputs - centre), axis=1, keepdims=True)
    normed = ((inputs - centre) * lax.rsqrt(spread + LN_EPS) * ln_gain + ln_shift).astype(
        jnp.bfloat16
    )
    return normed, inputs


def attend(same_image, head_count, joined):
    loaders, row_count, _ = same_image.shape
    width = joined.shape[1] // 3
    head_size = width // head_count

    def heads_of(part):
        return part.reshape(loaders, row_count, head_count, head_size).astype(jnp.float32)

    queries = heads_of(joined[:, :width])
    keys = heads_of(joined[:, width : 2 * width])
    values = heads_of(joined[:, 2 * width :])
    scores = jnp.einsum("aqhd,akhd->ahqk", queries, keys) * head_size ** (-0.5)
    scores = jnp.where(same_image[:, None], scores, NEG_FILL)
    row_peak = lax.stop_gradient(jnp.max(scores, axis=3, keepdims=True))
    exp_scores = jnp.exp(scores - row_peak)
    weights = (exp_scores / jnp.sum(exp_scores, axis=3, keepdims=True)).astype(jnp.bfloat16)
    context = jnp.einsum("ahqk,akhd->aqhd", weights.astype(jnp.float32), values)
    return context.reshape(loaders * row_count, width).astype(jnp.bfloat16)


def to_group(rows, dp_size):
    copies = jnp.broadcast_to(rows[None], (dp_size,) + rows.shape)
    return lax.all_to_all(copies, "dp", 0, 0, tiled=True).reshape(-1, rows.shape[1])


def per_device(tokens, patches, owners, ln_gain, ln_shift, w_qkv, b_qkv, w_proj, b_proj, grad_out):
    own_tokens = tokens[0]
    row_count, model_width = own_tokens.shape
    dp_size = lax.axis_size("dp")
    fsdp_size = lax.axis_size("fsdp")
    me = lax.axis_index("dp")
    shard = lax.axis_index("fsdp")
    head_count = HEADS // dp_size
    width = model_width // dp_size
    shard_rows = w_qkv.shape[0]

    w_part = jnp.concatenate(
        [
            lax.dynamic_slice_in_dim(w_qkv, part * model_width + me * width, width, 1)
            for part in range(3)
        ],
        axis=1,
    )
    b_part = lax.dynamic_slice_in_dim(b_qkv.reshape(3, dp_size, width), me, 1, axis=1).reshape(-1)

    piece_rows = shard_rows // dp_size
    per_block = width // shard_rows
    to_heads = [
        (d * fsdp_size + f, (f // per_block) * fsdp_size + (f % per_block) * dp_size + d)
        for d in range(dp_size)
        for f in range(fsdp_size)
    ]
    to_shards = [(there, here) for here, there in to_heads]
    own_piece = lax.dynamic_index_in_dim(
        w_proj.reshape(dp_size, piece_rows, model_width), me, 0, keepdims=False
    )
    head_piece = lax.ppermute(own_piece, ("dp", "fsdp"), to_heads)

    tables = lax.all_gather(
        jnp.concatenate([patches, owners], axis=2), "dp", axis=1, tiled=True
    )[0]
    own_tokens, tables = lax.optimization_barrier((own_tokens, tables))
    all_tokens = to_group(own_tokens, dp_size)
    weights = lax.all_gather(
        jnp.concatenate([w_part, head_piece.reshape(shard_rows, width)], axis=1),
        "fsdp",
        axis=0,
        tiled=True,
    )
    w_heads = weights[:, : 3 * width]
    w_rows = weights[:, 3 * width :].reshape(width, model_width)
    late_grad, all_tokens = lax.optimization_barrier((grad_out[0], all_tokens))
    all_grad = to_group(late_grad, dp_size)
    lengths, targets = tables[:, :dp_size], tables[:, dp_size:]

    positions = jnp.arange(row_count, dtype=jnp.int32)
    peers = jnp.arange(dp_size, dtype=jnp.int32)
    slot_start = jnp.cumsum(lengths, axis=1) - lengths
    slot_end = slot_start + lengths
    hits = (targets[:, :, None] == peers).astype(jnp.int32)
    pair_length = jnp.sum(lengths[:, :, None] * hits, axis=1)
    pair_start = jnp.sum(slot_start[:, :, None] * hits, axis=1)
    pair_offset = jnp.cumsum(pair_length, axis=0) - pair_length
    slot_base = (
        targets * row_count + jnp.sum(hits * pair_offset[:, None, :], axis=2) - slot_start
    )
    image = jnp.sum((positions[None, :, None] >= slot_end[:, None, :]).astype(jnp.int32), axis=2)
    image_hit = (image[:, :, None] == peers).astype(jnp.int32)
    destination = (
        jnp.sum(image_hit * slot_base[:, None, :], axis=2) + positions[None, :]
    ).reshape(-1)
    same_image = image[:, :, None] == image[:, None, :]
    pair_end = pair_offset + pair_length
    source = jnp.sum(
        (positions[None, :, None] >= pair_end.T[:, None, :]).astype(jnp.int32), axis=2
    )
    source_hit = (source[:, :, None] == peers).astype(jnp.int32)
    pair_base = (peers[:, None] * row_count + pair_start - pair_offset).T
    origin = jnp.sum(source_hit * pair_base[:, None, :], axis=2) + positions[None, :]

    normed, _ = layer_norm(all_tokens, ln_gain, ln_shift)
    joined = (jnp.dot(normed, w_heads, preferred_element_type=jnp.float32) + b_part).astype(
        jnp.bfloat16
    )
    context, attend_back = jax.vjp(partial(attend, same_image, head_count), joined)
    context, all_grad = lax.optimization_barrier((context, all_grad))
    grad_rows = all_grad[destination]
    grad_context = lax.dot_general(
        grad_rows, w_rows, (((1,), (1,)), ((), ())), preferred_element_type=jnp.float32
    ).astype(jnp.bfloat16)
    part_out = jnp.dot(
        context[origin.reshape(-1)], w_rows, preferred_element_type=jnp.float32
    ).astype(jnp.bfloat16)
    grad_context, part_out = lax.optimization_barrier((grad_context, part_out))
    parts_out = lax.all_to_all(
        part_out.reshape(dp_size, row_count, model_width), "dp", 0, 0, tiled=True
    )
    (grad_joined,) = attend_back(grad_context)

    term_proj = lax.dot_general(
        context, grad_rows, (((0,), (0,)), ((), ())), preferred_element_type=jnp.float32
    ).astype(jnp.bfloat16)
    pieces = lax.all_to_all(
        term_proj.reshape(fsdp_size, piece_rows, model_width), "fsdp", 0, 0, tiled=True
    )
    piece_proj = jnp.sum(pieces.astype(jnp.float32), axis=0).astype(jnp.bfloat16)
    piece_proj = lax.ppermute(piece_proj, ("dp", "fsdp"), to_shards)

    term_qkv = lax.dot_general(
        normed, grad_joined, (((0,), (0,)), ((), ())), preferred_element_type=jnp.float32
    ).astype(jnp.bfloat16)
    shard_qkv = lax.psum_scatter(term_qkv, "fsdp", scatter_dimension=0, tiled=True)
    sums = jnp.concatenate([shard_qkv, piece_proj.reshape(shard_rows, width)], axis=1)
    all_sums = lax.all_gather(sums, "dp", axis=0)
    all_qkv = all_sums[:, :, : 3 * width]
    summed_proj = all_sums[:, :, 3 * width :].reshape(shard_rows, model_width)
    summed_qkv = jnp.concatenate(
        [
            all_qkv[peer, :, part * width : (part + 1) * width]
            for part in range(3)
            for peer in range(dp_size)
        ],
        axis=1,
    )

    part_normed = lax.dot_general(
        grad_joined, w_heads, (((1,), (1,)), ((), ())), preferred_element_type=jnp.float32
    ).astype(jnp.bfloat16)
    part_normed, parts_out = lax.optimization_barrier((part_normed, parts_out))
    parts = lax.all_to_all(
        part_normed.reshape(dp_size, row_count, model_width), "dp", 0, 0, tiled=True
    )
    grad_normed = jnp.sum(parts.astype(jnp.float32), axis=0).astype(jnp.bfloat16)
    own_grad = lax.dynamic_slice_in_dim(grad_rows, me * row_count, row_count, 0).astype(
        jnp.float32
    )
    _, norm_back = jax.vjp(layer_norm, own_tokens, ln_gain, ln_shift)
    grad_tokens, gain_term, shift_term = norm_back((grad_normed, own_grad))

    own_origin = lax.dynamic_slice_in_dim(origin, me, 1, 0)[0]
    owned = all_tokens[own_origin].astype(jnp.float32)
    y_owned = (jnp.sum(parts_out.astype(jnp.float32), axis=0) + b_proj + owned).astype(
        jnp.bfloat16
    )

    bias_part = jnp.sum(grad_joined.astype(jnp.float32), axis=0).reshape(3, 1, width)
    bias_term = jnp.where(
        peers[None, :, None] == me, bias_part, jnp.zeros((), jnp.float32)
    ).reshape(-1)
    proj_term = jnp.sum(grad_out[0].astype(jnp.float32), axis=0)
    terms = jnp.concatenate([gain_term, shift_term, bias_term, proj_term])
    spread = lax.all_to_all(
        terms.reshape(dp_size * fsdp_size, -1), ("dp", "fsdp"), 0, 0, tiled=True
    )
    device_share = 1.0 / (dp_size * fsdp_size)
    share = jnp.sum(spread, axis=0, keepdims=True) * device_share
    small = lax.all_to_all(
        jnp.broadcast_to(share, spread.shape), ("dp", "fsdp"), 0, 0, tiled=True
    ).reshape(-1)
    cuts = (model_width, 2 * model_width, 5 * model_width)
    gain, shift, qkv_bias, proj_bias = jnp.split(small, cuts)
    return (
        y_owned[None],
        grad_tokens[None],
        summed_qkv.astype(jnp.float32) * device_share,
        summed_proj.astype(jnp.float32) * device_share,
        gain,
        shift,
        qkv_bias,
        proj_bias,
    )


def solution(mesh):
    placed = (
        P("fsdp", "dp", None),
        P("fsdp", "dp", None),
        P("fsdp", "dp", None),
        P(),
        P(),
        P("fsdp", None),
        P(),
        P("fsdp", None),
        P(),
        P("fsdp", "dp", None),
    )
    return jax.shard_map(
        per_device,
        mesh=mesh,
        in_specs=placed,
        out_specs=(
            P("fsdp", "dp", None),
            P("fsdp", "dp", None),
            P("fsdp", None),
            P("fsdp", None),
            P(),
            P(),
            P(),
            P(),
        ),
        check_vma=False,
    )
```
